256 devices in a mesh: rep: 16 (over y, z_lo), fsdp: 16 (over x, z_hi, core).
Axes of the slice: x: 4, y: 4, z: 8 (z_hi: 2, z_lo: 4; z = z_hi * 4 + z_lo), core: 2. Of those that a mesh axis runs over, the one named last changes fastest.
Arguments:
- hidden: bfloat16 [131072, 8192], P(('rep', 'fsdp')), may hold values from -6 to 6
- key_cotangent: bfloat16 [131072, 512], P(('rep', 'fsdp')), may hold values from -6 to 6
- local_weight: bfloat16 [16, 8192, 512], P('rep', 'fsdp'), may hold values from -0.0625 to 0.0625
- outer_delta: float32 [16, 8192, 512], P('rep', 'fsdp'), may hold values from -6 to 6
- global_params: float32 [2, 8192, 512], P(None, 'fsdp'), may hold values from -6 to 6
- momentum: float32 [2, 8192, 512], P(None, 'fsdp'), may hold values from -6 to 6
- outer_step: int32 [1], replicated, may hold values from 0 to 4095
Outputs:
- weight_grad: float32 [16, 8192, 512], P('rep', 'fsdp')
- new_global: float32 [8192, 512], P('fsdp')
- new_momentum: float32 [8192, 512], P('fsdp')
The draws below stay inside these ranges and needn't reach their ends.
All inputs are finite; a program needn't handle non-finite values.
Results may differ from the reference program's by a relative error of at most 0.0029.
Values may be sent and summed in bfloat16 or wider, within the bound.
No kernel may reach another device: no remote copies, remote signals or barrier semaphores. Data moves between devices by JAX's collectives and lax.ppermute only.
A program may use at most 128 MiB of HBM per device.

```python
import jax
import jax.numpy as jnp
from jax import lax

D = 8192
HEAD_DIM = 128
FRAGS = 2
TOK_DEV = 512
KVW = 512
ALL_TOK = 131072
N_REP = 16
N_FSDP = 16


def steps_of(key, shape, pieces, smallest, top_value):
    def one(position, parts):
        steps = jax.random.uniform(jax.random.fold_in(jax.random.fold_in(key, 6), position), (parts,), jnp.float32, smallest / len(pieces), top_value / len(pieces))
        return jnp.repeat(jnp.exp(steps), shape[position] // parts).reshape((-1,) + (1,) * (len(shape) - position - 1))

    factor_of = one(*pieces[0])
    for cut in pieces[1:]:
        factor_of = factor_of * one(*cut)
    return factor_of


def centred(rng, shape, spread, most, split=(), held_as=jnp.bfloat16):
    drawn = spread * jax.random.normal(rng, shape, jnp.float32)
    if split:
        drawn = drawn * steps_of(rng, shape, split, -0.22, 0.18)
    return jnp.clip(drawn, -most, most).astype(held_as)


def setup_inputs(seed: int = 0) -> dict:
    keys = jax.random.split(jax.random.key(seed), 8)
    return {
        "hidden": centred(keys[0], (ALL_TOK, D), 1.0, 6.0, ((0, 256),)),
        "key_cotangent": centred(keys[1], (ALL_TOK, KVW), 1.0, 6.0, ((0, 256),)),
        "local_weight": centred(keys[2], (N_REP, D, KVW), D ** -0.5, 0.0625, ((0, 16), (1, 16))),
        "outer_delta": centred(keys[3], (N_REP, D, KVW), 1.0, 6.0, ((0, 16), (1, 16)), jnp.float32),
        "global_params": centred(keys[4], (FRAGS, D, KVW), 1.0, 6.0, ((1, 16),), jnp.float32),
        "momentum": centred(keys[5], (FRAGS, D, KVW), 1.0, 6.0, ((1, 16),), jnp.float32),
        "outer_step": jax.random.randint(keys[6], (1,), 0, 4096).astype(jnp.int32),
    }


def backprop(projected, incoming_raw):
    tokens_here = projected.shape[0]
    per_head = projected.reshape(tokens_here, -1, HEAD_DIM)
    inverse_rms = lax.rsqrt(lax.optimization_barrier(jnp.mean(per_head * per_head, axis=-1, keepdims=True)) + 1e-06)
    normed = per_head * inverse_rms
    incoming = incoming_raw.astype(jnp.float32).reshape(tokens_here, -1, HEAD_DIM)
    along = lax.optimization_barrier(jnp.mean(incoming * normed, axis=-1, keepdims=True))
    return (inverse_rms * (incoming - normed * along)).reshape(tokens_here, -1).astype(jnp.bfloat16)

def reference(hidden, key_cotangent, local_weight, outer_delta, global_params, momentum, outer_step):
    group_tokens = TOK_DEV * N_FSDP

    def one_group(replica):
        group_rows = lax.dynamic_slice_in_dim(hidden, replica * group_tokens, group_tokens, 0)
        group_back = lax.dynamic_slice_in_dim(key_cotangent, replica * group_tokens, group_tokens, 0)
        weight = lax.dynamic_index_in_dim(local_weight, replica, 0, keepdims=False)
        projected = jnp.dot(group_rows, weight, preferred_element_type=jnp.float32)
        key_back = backprop(projected, group_back)
        return lax.dot_general(group_rows, key_back, (((0,), (0,)), ((), ())), preferred_element_type=jnp.float32)
    weight_grad = lax.map(one_group, jnp.arange(N_REP, dtype=jnp.int32))
    average = lax.optimization_barrier(jnp.sum(outer_delta, axis=0)) / N_REP
    fragment = (outer_step[0] % FRAGS).astype(jnp.int32)
    old_moment = lax.dynamic_index_in_dim(momentum, fragment, 0, keepdims=False)
    old_params = lax.dynamic_index_in_dim(global_params, fragment, 0, keepdims=False)
    new_momentum = 0.9 * old_moment + average
    new_global = old_params - 0.7 * (average + 0.9 * new_momentum)
    return (weight_grad, new_global, new_momentum)
```

```python
import functools

import jax
import jax.numpy as jnp
from jax import lax
from jax.sharding import PartitionSpec as P

HEAD_DIM = 128
FRAGS = 2
NX = 4
NY = 4
NZL = 4
F32 = jnp.float32
BF16 = jnp.bfloat16
NC = 2


def fsdp_perm(dx=0, dz=0, dc=0):
    pairs = []
    for f in range(16):
        x, z, c = f // 4, (f // 2) % 2, f % 2
        pairs.append((f, (((x + dx) % NX) * 2 + (z ^ dz)) * 2 + (c ^ dc)))
    return pairs


def rep_perm(dy=0, dz=0):
    pairs = []
    for r in range(16):
        y, z = r // NZL, r % NZL
        pairs.append((r, ((y + dy) % NY) * NZL + (z + dz) % NZL))
    return pairs


def send(value, **kw):
    return lax.ppermute(value, "fsdp", fsdp_perm(**kw))


def rep_send(value, **kw):
    return lax.ppermute(value, "rep", rep_perm(**kw))


def after(value, *others):
    return lax.optimization_barrier((value,) + others)[0]


def rows_dot(a, b):
    return lax.dot_general(a, b, (((0,), (0,)), ((), ())), preferred_element_type=F32)


def backprop(projected, incoming):
    inverse_rms = lax.rsqrt(jnp.mean(projected * projected, axis=-1, keepdims=True) + 1e-06)
    normed = projected * inverse_rms
    incoming = incoming.astype(F32)
    along = jnp.mean(incoming * normed, axis=-1, keepdims=True)
    return (inverse_rms * (incoming - normed * along)).astype(BF16)


def block(value, index, size):
    return lax.dynamic_slice_in_dim(value, index * size, size, 0)


def rep_sum(delta):
    r = lax.axis_index("rep")
    y, z = r // NZL, r % NZL
    n = delta.shape[0] // NY
    part = block(delta, y, n)
    for k in (1, 3, 2):
        part = part + rep_send(block(delta, (y + k) % NY, n), dy=k)
    m = n // NZL
    mine = block(part, z, m)
    for k in (1, 3, 2):
        mine = mine + rep_send(block(part, (z + k) % NZL, m), dz=k)
    average = (mine / (NY * NZL)).astype(BF16)
    ring = [average] + [rep_send(average, dz=-k) for k in (1, 2, 3)]
    ring = jnp.stack(ring)
    part = jnp.concatenate([lax.dynamic_index_in_dim(ring, (k - z) % NZL, 0, keepdims=False) for k in range(NZL)])
    ring = jnp.stack([part] + [rep_send(part, dy=-k) for k in (1, 2, 3)])
    return jnp.concatenate([lax.dynamic_index_in_dim(ring, (k - y) % NY, 0, keepdims=False) for k in range(NY)]).astype(F32)


def per_device(hidden, key_cotangent, local_weight, outer_delta, global_params, momentum, outer_step):
    f = lax.axis_index("fsdp")
    x, zh, core = f // 4, (f // 2) % 2, f % 2
    weight = local_weight[0]
    rows, width = weight.shape
    half = width // 2
    chip_rows = 2 * rows
    chip_of = lambda dx, dz: ((x + dx) % NX) * 2 + (zh ^ dz)

    def mine(a):
        return lax.dynamic_slice_in_dim(a, core * half, half, 1)

    def theirs(a):
        return lax.dynamic_slice_in_dim(a, (1 - core) * half, half, 1)

    def in_order(own, other):
        return jnp.where(core == 0, jnp.concatenate([own, other]), jnp.concatenate([other, own]))

    w_here = in_order(mine(weight), send(theirs(weight), dc=1))
    hidden_sib = send(hidden, dc=1)
    cot = jnp.concatenate([mine(key_cotangent), send(theirs(key_cotangent), dc=1)])

    cols = half // NC
    gathered = [dict() for _ in range(NC)]
    for j in range(NC):
        here = w_here[:, j * cols : (j + 1) * cols]
        there = send(here, dz=1)
        for dz, piece in ((0, here), (1, there)):
            left = send(piece, dx=1)
            right = send(piece, dx=-1)
            far = jnp.concatenate([send(left[:rows], dx=1), send(right[rows:], dx=-1)])
            gathered[j][0, dz] = piece
            gathered[j][3, dz] = left
            gathered[j][1, dz] = right
            gathered[j][2, dz] = far

    acts = {}
    for dx in range(NX):
        for dz in range(2):
            start = chip_of(dx, dz) * chip_rows
            acts[dx, dz] = jnp.concatenate(
                [lax.dynamic_slice_in_dim(h, start, chip_rows, 1) for h in (hidden, hidden_sib)]
            )

    average = rep_sum(outer_delta[0])

    grads = []
    for j in range(NC):
        total = None
        for d in ((0, 0), (1, 0), (3, 0), (2, 0), (0, 1), (1, 1), (3, 1), (2, 1)):
            term = jnp.dot(acts[d], gathered[j][d], preferred_element_type=F32)
            total = term if total is None else total + term
        back = []
        for h in range(cols // HEAD_DIM):
            s = slice(h * HEAD_DIM, (h + 1) * HEAD_DIM)
            g = slice(j * cols + h * HEAD_DIM, j * cols + (h + 1) * HEAD_DIM)
            back.append(backprop(total[:, s], cot[:, g]))
        back = jnp.concatenate(back, axis=1) if len(back) > 1 else back[0]

        def ring(dz):
            far = rows_dot(acts[2, dz], back).astype(BF16)
            up = send(far[:rows], dx=1)
            down = send(far[rows:], dx=-1)
            right = rows_dot(acts[1, dz], back)
            left = rows_dot(acts[3, dz], back)
            right = jnp.concatenate([right[:rows] + up.astype(F32), right[rows:]]).astype(BF16)
            left = jnp.concatenate([left[:rows], left[rows:] + down.astype(F32)]).astype(BF16)
            return rows_dot(acts[0, dz], back) + send(right, dx=1).astype(F32) + send(left, dx=-1).astype(F32)

        away = send(ring(1).astype(BF16), dz=1)
        grads.append(ring(0) + away.astype(F32))
    grad = jnp.concatenate(grads, axis=1)
    own = block(grad, core, rows)
    other = send(block(grad, 1 - core, rows), dc=1)
    grad = jnp.where(core == 0, jnp.concatenate([own, other], 1), jnp.concatenate([other, own], 1))

    fragment = outer_step[0] % FRAGS
    old_moment = lax.dynamic_index_in_dim(momentum, fragment, 0, keepdims=False)
    old_params = lax.dynamic_index_in_dim(global_params, fragment, 0, keepdims=False)
    new_momentum = 0.9 * old_moment + average
    new_global = old_params - 0.7 * (average + 0.9 * new_momentum)
    return (grad[None], new_global, new_momentum)


def solution(mesh):
    in_specs = (
        P(("rep", "fsdp"), None),
        P(("rep", "fsdp"), None),
        P("rep", "fsdp", None),
        P("rep", "fsdp", None),
        P(None, "fsdp", None),
        P(None, "fsdp", None),
        P(),
    )
    out_specs = (P("rep", "fsdp", None), P("fsdp", None), P("fsdp", None))
    return jax.shard_map(
        per_device, mesh=mesh, in_specs=in_specs, out_specs=out_specs, check_vma=False
    )
```

```python
import jax
import jax.numpy as jnp
from jax import lax
from jax.experimental import pallas as pl
from jax.experimental.pallas import tpu as pltpu
from jax.sharding import PartitionSpec as P

HEAD_DIM = 128
FRAGS = 2
NX = 4
NY = 4
NZL = 4
F32 = jnp.float32
BF16 = jnp.bfloat16


def fsdp_perm(dx=0, dz=0, dc=0):
    pairs = []
    for f in range(16):
        x, z, c = f // 4, (f // 2) % 2, f % 2
        pairs.append((f, (((x + dx) % NX) * 2 + (z ^ dz)) * 2 + (c ^ dc)))
    return pairs


def rep_perm(dy=0, dz=0):
    pairs = []
    for r in range(16):
        y, z = r // NZL, r % NZL
        pairs.append((r, ((y + dy) % NY) * NZL + (z + dz) % NZL))
    return pairs


def send(value, **kw):
    return lax.ppermute(value, "fsdp", fsdp_perm(**kw))


def rep_send(value, **kw):
    return lax.ppermute(value, "rep", rep_perm(**kw))


def tie(*values):
    return lax.optimization_barrier(values)


ORDER = (2, 1, 3, 0)
TILE = 256
PARAMS = pltpu.CompilerParams(vmem_limit_bytes=48 * 1024 * 1024)


def rows_dot(a, b):
    return lax.dot_general(a, b, (((0,), (0,)), ((), ())), preferred_element_type=F32)


def backprop(projected, incoming):
    inverse_rms = lax.rsqrt(jnp.mean(projected * projected, axis=-1, keepdims=True) + 1e-06)
    normed = projected * inverse_rms
    incoming = incoming.astype(F32)
    along = jnp.mean(incoming * normed, axis=-1, keepdims=True)
    return (inverse_rms * (incoming - normed * along)).astype(BF16)


def forward_kernel(at_ref, own_ref, sib_ref, *refs):
    weights, out_ref = refs[:-1], refs[-1]
    step = pl.program_id(0)
    tokens = own_ref.shape[0]
    for i, w_ref in enumerate(weights):

        @pl.when(step == i)
        def _():
            for t, h_ref in enumerate((own_ref, sib_ref)):

                for n in range(0, tokens, TILE):
                    term = jnp.dot(h_ref[pl.ds(n, TILE), :], w_ref[...], preferred_element_type=F32)
                    where = pl.ds(t * tokens + n, TILE)
                    if i == 0:
                        out_ref[where, :] = term
                    else:
                        out_ref[where, :] += term


def forward_call(at, own, sib, weights):
    tokens = own.shape[0]
    depth, cols = weights[0].shape
    acts = pl.BlockSpec((tokens, depth), lambda i, at: (0, at[i]))
    whole = pl.BlockSpec((depth, cols), lambda i, at: (0, 0))
    return pl.pallas_call(
        forward_kernel,
        grid_spec=pltpu.PrefetchScalarGridSpec(
            num_scalar_prefetch=1,
            grid=(len(weights),),
            in_specs=[acts, acts] + [whole] * len(weights),
            out_specs=pl.BlockSpec((2 * tokens, cols), lambda i, at: (0, 0)),
        ),
        out_shape=jax.ShapeDtypeStruct((2 * tokens, cols), F32),
        compiler_params=PARAMS,
        cost_estimate=pl.CostEstimate(
            flops=16 * tokens * depth * cols, bytes_accessed=16 * tokens * depth, transcendentals=0
        ),
        name="own_forward",
    )(at, own, sib, *weights)


def middle_kernel(at_ref, own_ref, sib_ref, part_ref, cot_ref, *refs):
    weights, (back_ref, *outs), (held, acc, sems) = refs[:4], refs[4:9], refs[9:]
    tokens = own_ref.shape[0]
    depth = held.shape[2]

    def copy(i, t):
        start = pl.multiple_of(at_ref[i] * depth, depth)
        return pltpu.make_async_copy(
            (own_ref, sib_ref)[t].at[:, pl.ds(start, depth)],
            held.at[i, pl.ds(t * tokens, tokens), :],
            sems.at[i, t],
        )

    for i in range(4):
        for t in range(2):
            copy(i, t).start()
    for i in range(4):
        for t in range(2):
            copy(i, t).wait()

        for n in range(0, 2 * tokens, TILE):
            where = pl.ds(n, TILE)
            term = jnp.dot(held[i, where, :], weights[i][...], preferred_element_type=F32)
            if i == 0:
                acc[where, :] = part_ref[where, :] + term
            else:
                acc[where, :] += term

    for n in range(0, 2 * tokens, TILE):
        where = pl.ds(n, TILE)
        for h in range(0, acc.shape[1], HEAD_DIM):
            head = pl.ds(h, HEAD_DIM)
            back_ref[where, head] = backprop(acc[where, head], cot_ref[where, head])

    for i in range(4):
        for n in range(0, depth, TILE):
            where = pl.ds(n, TILE)
            outs[i][where, :] = rows_dot(held[i, :, where], back_ref[...]).astype(outs[i].dtype)


def middle_call(at, own, sib, part, cot, weights):
    tokens = own.shape[0]
    depth, cols = weights[0].shape
    vmem = pl.BlockSpec(memory_space=pltpu.VMEM)
    hbm = pl.BlockSpec(memory_space=pl.ANY)
    return pl.pallas_call(
        middle_kernel,
        in_specs=[pl.BlockSpec(memory_space=pltpu.SMEM), hbm, hbm] + [vmem] * 6,
        out_specs=[vmem] * 5,
        out_shape=[jax.ShapeDtypeStruct((2 * tokens, cols), BF16)]
        + [jax.ShapeDtypeStruct((depth, cols), t) for t in (BF16, BF16, BF16, F32)],
        scratch_shapes=[
            pltpu.VMEM((4, 2 * tokens, depth), BF16),
            pltpu.VMEM((2 * tokens, cols), F32),
            pltpu.SemaphoreType.DMA((4, 2)),
        ],
        compiler_params=PARAMS,
        cost_estimate=pl.CostEstimate(
            flops=32 * tokens * depth * cols, bytes_accessed=16 * tokens * depth, transcendentals=0
        ),
        name="middle",
    )(at, own, sib, part, cot, *weights)


def gradient_kernel(at_ref, own_ref, sib_ref, back_ref, *outs):
    step = pl.program_id(0)
    tokens, depth = own_ref.shape
    for i, out_ref in enumerate(outs):

        @pl.when(step == i)
        def _():
            for n in range(0, depth, TILE):
                where = pl.ds(n, TILE)
                term = rows_dot(own_ref[:, where], back_ref[:tokens, :])
                term += rows_dot(sib_ref[:, where], back_ref[tokens:, :])
                out_ref[where, :] = term.astype(out_ref.dtype)


def gradient_call(at, own, sib, back, depth):
    tokens = own.shape[0]
    cols = back.shape[1]
    acts = pl.BlockSpec((tokens, depth), lambda i, at: (0, at[i]))
    whole = lambda r: pl.BlockSpec((r, cols), lambda i, at: (0, 0))
    return pl.pallas_call(
        gradient_kernel,
        grid_spec=pltpu.PrefetchScalarGridSpec(
            num_scalar_prefetch=1,
            grid=(4,),
            in_specs=[acts, acts, whole(2 * tokens)],
            out_specs=[whole(depth)] * 4,
        ),
        out_shape=[jax.ShapeDtypeStruct((depth, cols), t) for t in (BF16, BF16, BF16, F32)],
        compiler_params=PARAMS,
        cost_estimate=pl.CostEstimate(
            flops=16 * tokens * depth * cols, bytes_accessed=16 * tokens * depth, transcendentals=0
        ),
        name="gradient",
    )(at, own, sib, back)


def block(value, index, size):
    return lax.dynamic_slice_in_dim(value, index * size, size, 0)


def rep_blocks(delta):
    y = lax.axis_index("rep") // NZL
    n = delta.shape[0] // NY
    return [block(delta, (y + k) % NY, n) for k in range(NY)]


def rep_rows(blocks):
    part = blocks[0]
    for k in (1, 3, 2):
        part = part + rep_send(blocks[k], dy=k)
    return part


def rep_average(part):
    z = lax.axis_index("rep") % NZL
    m = part.shape[0] // NZL
    mine = block(part, z, m)
    for k in (1, 3, 2):
        mine = mine + rep_send(block(part, (z + k) % NZL, m), dz=k)
    return (mine / (NY * NZL)).astype(BF16)


def rep_gather_z(average):
    z = lax.axis_index("rep") % NZL
    ring = jnp.stack([average] + [rep_send(average, dz=-k) for k in (1, 2, 3)])
    return jnp.concatenate([lax.dynamic_index_in_dim(ring, (k - z) % NZL, 0, keepdims=False) for k in range(NZL)])


def rep_gather_y(part):
    y = lax.axis_index("rep") // NZL
    ring = jnp.stack([part] + [rep_send(part, dy=-k) for k in (1, 2, 3)])
    return jnp.concatenate([lax.dynamic_index_in_dim(ring, (k - y) % NY, 0, keepdims=False) for k in range(NY)])


def per_device(hidden, key_cotangent, local_weight, outer_delta, global_params, momentum, outer_step):
    f = lax.axis_index("fsdp")
    x, zh, core = f // 4, (f // 2) % 2, f % 2
    weight = local_weight[0]
    rows, width = weight.shape
    half = width // 2
    chip_rows = 2 * rows
    chip_of = lambda dx, dz: ((x + dx) % NX) * 2 + (zh ^ dz)

    def mine(a):
        return lax.dynamic_slice_in_dim(a, core * half, half, 1)

    def theirs(a):
        return lax.dynamic_slice_in_dim(a, (1 - core) * half, half, 1)

    def in_order(own, other):
        return jnp.where(core == 0, jnp.concatenate([own, other]), jnp.concatenate([other, own]))

    from_sib = send(theirs(weight), dc=1)
    cot_sib = send(theirs(key_cotangent), dc=1)
    blocks = rep_blocks(outer_delta[0])
    here = in_order(mine(weight), from_sib)

    def spread(piece):
        return {0: piece, 3: send(piece, dx=1), 1: send(piece, dx=-1), 2: send(piece, dx=2)}

    away = send(here, dz=1)
    gathered = spread(here)
    here, *blocks = tie(here, *blocks)
    part = rep_rows(blocks)
    away, *gathered, part, hidden = tie(away, *[gathered[dx] for dx in ORDER], part, hidden)
    distant = spread(away)
    hidden_sib = send(hidden, dc=1)
    average = rep_average(part)
    at = lambda dz: jnp.stack([chip_of(dx, dz) for dx in ORDER]).astype(jnp.int32)
    partial = forward_call(at(0), hidden, hidden_sib, gathered)
    partial, average, *distant = tie(partial, average, *[distant[dx] for dx in ORDER])
    cots = jnp.concatenate([mine(key_cotangent), cot_sib])
    back, *found = middle_call(at(1), hidden, hidden_sib, partial, cots, distant)

    def gather(found):
        return [send(found[0], dx=2), send(found[1], dx=1), send(found[2], dx=-1), found[3]]

    def total(found):
        return found[3] + (found[1].astype(F32) + found[2].astype(F32)) + found[0].astype(F32)

    first = gather(found)
    back, average = tie(back, average)
    local = gradient_call(at(0), hidden, hidden_sib, back, chip_rows)
    average = rep_gather_z(average)
    *both, average = tie(*first, *local, average)
    away = send(total(both[:4]).astype(BF16), dz=1)
    local = gather(both[4:])
    average = rep_gather_y(average).astype(F32)
    fragment = outer_step[0] % FRAGS
    old_moment = lax.dynamic_index_in_dim(momentum, fragment, 0, keepdims=False)
    old_params = lax.dynamic_index_in_dim(global_params, fragment, 0, keepdims=False)
    new_momentum = 0.9 * old_moment + average
    new_global = old_params - 0.7 * (average + 0.9 * new_momentum)
    new_momentum, new_global, away, *local = tie(new_momentum, new_global, away, *local)
    local = total(local) + away.astype(F32)
    own = block(local, core, rows)
    other = send(block(local, 1 - core, rows), dc=1)
    grad = jnp.where(core == 0, jnp.concatenate([own, other], 1), jnp.concatenate([other, own], 1))

    return (grad[None], new_global, new_momentum)


def solution(mesh):
    in_specs = (
        P(("rep", "fsdp"), None),
        P(("rep", "fsdp"), None),
        P("rep", "fsdp", None),
        P("rep", "fsdp", None),
        P(None, "fsdp", None),
        P(None, "fsdp", None),
        P(),
    )
    out_specs = (P("rep", "fsdp", None), P("fsdp", None), P("fsdp", None))
    return jax.shard_map(
        per_device, mesh=mesh, in_specs=in_specs, out_specs=out_specs, check_vma=False
    )
```

```python
import jax
import jax.numpy as jnp
from jax import lax
from jax.experimental import pallas as pl
from jax.experimental.pallas import tpu as pltpu
from jax.sharding import PartitionSpec as P

HEAD_DIM = 128
FRAGS = 2
NX = 4
NY = 4
NZL = 4
F32 = jnp.float32
BF16 = jnp.bfloat16


def fsdp_perm(dx=0, dz=0, dc=0):
    pairs = []
    for f in range(16):
        x, z, c = f // 4, (f // 2) % 2, f % 2
        pairs.append((f, (((x + dx) % NX) * 2 + (z ^ dz)) * 2 + (c ^ dc)))
    return pairs


def rep_perm(dy=0, dz=0):
    pairs = []
    for r in range(16):
        y, z = r // NZL, r % NZL
        pairs.append((r, ((y + dy) % NY) * NZL + (z + dz) % NZL))
    return pairs


def flip_perm(bit):
    return [(r, (r // NZL ^ bit) * NZL + r % NZL) for r in range(16)]


def send(value, **kw):
    return lax.ppermute(value, "fsdp", fsdp_perm(**kw))


def rep_send(value, **kw):
    return lax.ppermute(value, "rep", rep_perm(**kw))


def tie(*values):
    return lax.optimization_barrier(values)


ORDER = (2, 1, 3, 0)
TILE = 256
PARAMS = pltpu.CompilerParams(vmem_limit_bytes=22 * 1024 * 1024)


def rows_dot(a, b):
    return lax.dot_general(a, b, (((0,), (0,)), ((), ())), preferred_element_type=F32)


def backprop(projected, incoming):
    inverse_rms = lax.rsqrt(jnp.mean(projected * projected, axis=-1, keepdims=True) + 1e-06)
    normed = projected * inverse_rms
    incoming = incoming.astype(F32)
    along = jnp.mean(incoming * normed, axis=-1, keepdims=True)
    return (inverse_rms * (incoming - normed * along)).astype(BF16)


def forward_kernel(at_ref, own_ref, sib_ref, *refs):
    weights, (out_ref, held, acts, sems) = refs[:4], refs[4:]
    tokens = own_ref.shape[0]
    depth = held.shape[2]

    def copy(i, t):
        start = pl.multiple_of(at_ref[i] * depth, depth)
        kept = (acts if i < 4 else held).at[i % 4, pl.ds(t * tokens, tokens), :]
        return pltpu.make_async_copy((own_ref, sib_ref)[t].at[:, pl.ds(start, depth)], kept, sems.at[i, t])

    for i in range(8):
        for t in range(2):
            copy(i, t).start()
    for i in range(4):
        for t in range(2):
            copy(i, t).wait()
        for n in range(0, 2 * tokens, TILE):
            where = pl.ds(n, TILE)
            term = jnp.dot(acts[i, where, :], weights[i][...], preferred_element_type=F32)
            if i == 0:
                out_ref[where, :] = term
            else:
                out_ref[where, :] += term
    for i in range(4, 8):
        for t in range(2):
            copy(i, t).wait()


def forward_call(at, own, sib, weights):
    tokens = own.shape[0]
    depth, cols = weights[0].shape
    vmem = pl.BlockSpec(memory_space=pltpu.VMEM)
    hbm = pl.BlockSpec(memory_space=pltpu.HBM)
    return pl.pallas_call(
        forward_kernel,
        in_specs=[pl.BlockSpec(memory_space=pltpu.SMEM), hbm, hbm] + [vmem] * 4,
        out_specs=[vmem, vmem],
        out_shape=[
            jax.ShapeDtypeStruct((2 * tokens, cols), F32),
            jax.ShapeDtypeStruct((4, 2 * tokens, depth), BF16),
        ],
        scratch_shapes=[pltpu.VMEM((4, 2 * tokens, depth), BF16), pltpu.SemaphoreType.DMA((8, 2))],
        compiler_params=PARAMS,
        cost_estimate=pl.CostEstimate(
            flops=16 * tokens * depth * cols, bytes_accessed=0, transcendentals=0
        ),
        name="own_forward",
    )(at, own, sib, *weights)


def middle_kernel(held, part_ref, cot_ref, *refs):
    weights, (back_ref, *outs), acc = refs[:8], refs[8:16], refs[16]
    tokens = held.shape[1] // 2
    depth = held.shape[2]
    for i in range(4):
        for n in range(0, 2 * tokens, TILE):
            where = pl.ds(n, TILE)
            term = sum(
                jnp.dot(held[i, where, pl.ds(h * depth // 2, depth // 2)], weights[2 * i + h][...], preferred_element_type=F32)
                for h in range(2)
            )
            if i == 0:
                acc[where, :] = part_ref[where, :] + term
            else:
                acc[where, :] += term

    for n in range(0, 2 * tokens, TILE):
        where = pl.ds(n, TILE)
        for h in range(0, acc.shape[1], HEAD_DIM):
            head = pl.ds(h, HEAD_DIM)
            back_ref[where, head] = backprop(acc[where, head], cot_ref[where, head])

    for i in range(4):
        for n in range(0, depth, TILE):
            term = rows_dot(held[i, :, pl.ds(n, TILE)], back_ref[...])
            if i == 3:
                outs[6][pl.ds(n, TILE), :] = term
            else:
                out_ref = outs[2 * i + n // (depth // 2)]
                out_ref[pl.ds(n % (depth // 2), TILE), :] = term.astype(out_ref.dtype)


def middle_call(held, part, cot, weights):
    tokens, depth = held.shape[1] // 2, held.shape[2]
    cols = weights[0].shape[1]
    halves = (BF16, BF16, F32, BF16, BF16, F32)
    vmem = pl.BlockSpec(memory_space=pltpu.VMEM)
    return pl.pallas_call(
        middle_kernel,
        in_specs=[vmem] * 11,
        out_specs=[vmem] * 8,
        out_shape=[jax.ShapeDtypeStruct((2 * tokens, cols), BF16)]
        + [jax.ShapeDtypeStruct((depth // 2, cols), t) for t in halves]
        + [jax.ShapeDtypeStruct((depth, cols), F32)],
        scratch_shapes=[pltpu.VMEM((2 * tokens, cols), F32)],
        compiler_params=PARAMS,
        cost_estimate=pl.CostEstimate(
            flops=32 * tokens * depth * cols, bytes_accessed=0, transcendentals=0
        ),
        name="middle",
    )(held, part, cot, *weights)


def gradient_kernel(at_ref, own_ref, sib_ref, back_ref, *refs):
    outs, (acts, sems) = refs[:4], refs[4:]
    tokens = own_ref.shape[0]
    depth = acts.shape[2]

    def copy(i, t):
        start = pl.multiple_of(at_ref[i] * depth, depth)
        kept = acts.at[i, pl.ds(t * tokens, tokens), :]
        return pltpu.make_async_copy((own_ref, sib_ref)[t].at[:, pl.ds(start, depth)], kept, sems.at[i, t])

    for i in range(4):
        for t in range(2):
            copy(i, t).start()
    for i in range(4):
        for t in range(2):
            copy(i, t).wait()
        for n in range(0, depth, TILE):
            where = pl.ds(n, TILE)
            outs[i][where, :] = rows_dot(acts[i, :, where], back_ref[...]).astype(outs[i].dtype)


def gradient_call(at, own, sib, back, depth):
    tokens = own.shape[0]
    cols = back.shape[1]
    vmem = pl.BlockSpec(memory_space=pltpu.VMEM)
    hbm = pl.BlockSpec(memory_space=pltpu.HBM)
    return pl.pallas_call(
        gradient_kernel,
        in_specs=[pl.BlockSpec(memory_space=pltpu.SMEM), hbm, hbm, vmem],
        out_specs=[vmem] * 4,
        out_shape=[jax.ShapeDtypeStruct((depth, cols), t) for t in (BF16, BF16, BF16, F32)],
        scratch_shapes=[pltpu.VMEM((4, 2 * tokens, depth), BF16), pltpu.SemaphoreType.DMA((4, 2))],
        compiler_params=PARAMS,
        cost_estimate=pl.CostEstimate(
            flops=16 * tokens * depth * cols, bytes_accessed=0, transcendentals=0
        ),
        name="gradient",
    )(at, own, sib, back)


def block(value, index, size):
    return lax.dynamic_slice_in_dim(value, index * size, size, 0)


def rep_halves(value, bit):
    n = value.shape[0] // 2
    return block(value, bit, n), block(value, 1 - bit, n).astype(BF16)


def rep_rows(delta):
    y = lax.axis_index("rep") // NZL
    for bit in (1, 2):
        kept, given = rep_halves(delta, (y // bit) % 2)
        delta = kept, lax.ppermute(given, "rep", flip_perm(bit))
        if bit == 1:
            delta = delta[0] + delta[1].astype(F32)
    return delta


def rep_parts(pieces):
    part = pieces[0] + pieces[1].astype(F32)
    z = lax.axis_index("rep") % NZL
    m = part.shape[0] // NZL
    return [block(part, z, m)] + [rep_send(block(part, (z + k) % NZL, m), dz=k) for k in (1, 2, 3)]


def rep_average(pieces):
    total = pieces[0] + pieces[1] + pieces[3] + pieces[2]
    average = (total / (NY * NZL)).astype(BF16)
    return [average] + [rep_send(average, dz=-k) for k in (1, 2, 3)]


def ordered(pieces, index, holders):
    ring = jnp.stack(pieces)
    n = len(pieces)
    return jnp.concatenate([lax.dynamic_index_in_dim(ring, (k - index) % n, 0, keepdims=False) for k in holders])


def rep_gather(pieces):
    part = ordered(pieces, lax.axis_index("rep") % NZL, range(NZL))
    return [part] + [rep_send(part, dy=-k) for k in (1, 2, 3)]


def per_device(hidden, key_cotangent, local_weight, outer_delta, global_params, momentum, outer_step):
    f = lax.axis_index("fsdp")
    x, zh, core = f // 4, (f // 2) % 2, f % 2
    weight = local_weight[0]
    rows, width = weight.shape
    half = width // 2
    chip_rows = 2 * rows
    chip_of = lambda dx, dz: ((x + dx) % NX) * 2 + (zh ^ dz)

    def mine(a):
        return lax.dynamic_slice_in_dim(a, core * half, half, 1)

    def theirs(a):
        return lax.dynamic_slice_in_dim(a, (1 - core) * half, half, 1)

    def in_order(own, other):
        return jnp.where(core == 0, jnp.concatenate([own, other]), jnp.concatenate([other, own]))

    from_sib = send(jnp.concatenate([theirs(weight), theirs(key_cotangent)]), dc=1)
    cots = jnp.concatenate([mine(key_cotangent), from_sib[rows:]])
    here = in_order(mine(weight), from_sib[:rows])

    def spread(piece):
        return {0: piece, 3: send(piece, dx=1), 1: send(piece, dx=-1), 2: send(piece, dx=2)}

    away = send(here, dz=1)
    gathered = spread(here)
    far, right, left, away, here, cots, hidden, *blocks = tie(
        gathered[2], gathered[1], gathered[3], away, here, cots, hidden, *rep_rows(outer_delta[0])
    )
    gathered = [far, right, left, here]
    top, bottom = away[:rows], away[rows:]
    from_left, from_right = send(top, dx=1), send(bottom, dx=-1)
    far = [send(from_left, dx=1), send(from_right, dx=-1)]
    distant = [*far, send(top, dx=-1), from_right, from_left, send(bottom, dx=1), top, bottom]
    hidden_sib = send(hidden, dc=1)
    blocks = rep_parts(blocks)
    at = lambda dz: jnp.stack([chip_of(dx, dz) for dx in ORDER]).astype(jnp.int32)
    both = jnp.concatenate([at(0), at(1)])
    partial, held = forward_call(both, hidden, hidden_sib, gathered)
    partial, held, *rest = tie(partial, held, *distant, *blocks)
    distant, blocks = rest[:8], rest[8:]
    back, *found = middle_call(held, partial, cots, distant)

    def gather(found):
        return [send(found[0], dx=2), send(found[1], dx=1), send(found[2], dx=-1), found[3]]

    def total(found):
        found = [v.astype(F32) for v in found]
        return found[3] + (found[1] + found[2]) + found[0]

    up, down = send(found[0], dx=1), send(found[1], dx=-1)
    bottom, top = send(found[3], dx=1), send(found[4], dx=-1)
    up = send((found[2] + up.astype(F32)).astype(BF16), dx=1)
    down = send((found[5] + down.astype(F32)).astype(BF16), dx=-1)
    first = (up, down, bottom, top, found[6])
    back, *blocks = tie(back, *blocks)
    local = gradient_call(at(0), hidden, hidden_sib, back, chip_rows)
    rest = tie(*first, *local, *rep_average(blocks))
    (up, down, bottom, top, mid), local, blocks = rest[:5], rest[5:9], rest[9:]
    added = jnp.concatenate([up.astype(F32) + top.astype(F32), bottom.astype(F32) + down.astype(F32)])
    away = send((mid + added).astype(BF16), dz=1)
    local = gather(local)
    summed = [total([block(v, index, rows) for v in local]) for index in (core, 1 - core)]
    here, there, away, *blocks = tie(*summed, away, *rep_gather(blocks))
    finish = [v + block(away, index, rows).astype(F32) for v, index in zip((here, there), (core, 1 - core))]
    own, other = finish[0], send(finish[1], dc=1)
    average = ordered(blocks, lax.axis_index("rep") // NZL, (0, 2, 1, 3)).astype(F32)
    fragment = outer_step[0] % FRAGS
    old_moment = lax.dynamic_index_in_dim(momentum, fragment, 0, keepdims=False)
    old_params = lax.dynamic_index_in_dim(global_params, fragment, 0, keepdims=False)
    new_momentum = 0.9 * old_moment + average
    new_global = old_params - 0.7 * (average + 0.9 * new_momentum)
    grad = jnp.where(core == 0, jnp.concatenate([own, other], 1), jnp.concatenate([other, own], 1))

    return (grad[None], new_global, new_momentum)


def solution(mesh):
    in_specs = (
        P(("rep", "fsdp"), None),
        P(("rep", "fsdp"), None),
        P("rep", "fsdp", None),
        P("rep", "fsdp", None),
        P(None, "fsdp", None),
        P(None, "fsdp", None),
        P(),
    )
    out_specs = (P("rep", "fsdp", None), P("fsdp", None), P("fsdp", None))
    return jax.shard_map(
        per_device, mesh=mesh, in_specs=in_specs, out_specs=out_specs, check_vma=False
    )
```

```python
import jax
import jax.numpy as jnp
from jax import lax
from jax.experimental import pallas as pl
from jax.experimental.pallas import tpu as pltpu
from jax.sharding import PartitionSpec as P

HEAD_DIM = 128
FRAGS = 2
NX = 4
NY = 4
NZL = 4
F32 = jnp.float32
BF16 = jnp.bfloat16


def fsdp_perm(dx=0, dz=0, dc=0):
    pairs = []
    for f in range(16):
        x, z, c = f // 4, (f // 2) % 2, f % 2
        pairs.append((f, (((x + dx) % NX) * 2 + (z ^ dz)) * 2 + (c ^ dc)))
    return pairs


def rep_perm(dy=0, dz=0):
    pairs = []
    for r in range(16):
        y, z = r // NZL, r % NZL
        pairs.append((r, ((y + dy) % NY) * NZL + (z + dz) % NZL))
    return pairs


def flip_perm(bit):
    return [(r, (r // NZL ^ bit) * NZL + r % NZL) for r in range(16)]


def send(value, **kw):
    return lax.ppermute(value, "fsdp", fsdp_perm(**kw))


def rep_send(value, **kw):
    return lax.ppermute(value, "rep", rep_perm(**kw))


def tie(*values):
    return lax.optimization_barrier(values)


ORDER = (2, 1, 3, 0)
TILE = 256
PARAMS = pltpu.CompilerParams(vmem_limit_bytes=22 * 1024 * 1024)


def rows_dot(a, b):
    return lax.dot_general(a, b, (((0,), (0,)), ((), ())), preferred_element_type=F32)


def backprop(projected, incoming):
    inverse_rms = lax.rsqrt(jnp.mean(projected * projected, axis=-1, keepdims=True) + 1e-06)
    normed = projected * inverse_rms
    incoming = incoming.astype(F32)
    along = jnp.mean(incoming * normed, axis=-1, keepdims=True)
    return (inverse_rms * (incoming - normed * along)).astype(BF16)


def forward_kernel(at_ref, acts_ref, *refs):
    weights, (out_ref, held, acts, sems) = refs[:4], refs[4:]
    depth = held.shape[2]

    def copy(i):
        start = pl.multiple_of(at_ref[i] * depth, depth)
        kept = (acts if i < 4 else held).at[i % 4]
        return pltpu.make_async_copy(acts_ref.at[:, pl.ds(start, depth)], kept, sems.at[i])

    for i in range(8):
        copy(i).start()
    for i in range(4):
        copy(i).wait()
        for n in range(0, out_ref.shape[0], TILE):
            where = pl.ds(n, TILE)
            term = jnp.dot(acts[i, where, :], weights[i][...], preferred_element_type=F32)
            if i == 0:
                out_ref[where, :] = term
            else:
                out_ref[where, :] += term
    for i in range(4, 8):
        copy(i).wait()


def forward_call(at, acts, weights):
    tokens = acts.shape[0]
    depth, cols = weights[0].shape
    vmem = pl.BlockSpec(memory_space=pltpu.VMEM)
    hbm = pl.BlockSpec(memory_space=pltpu.HBM)
    return pl.pallas_call(
        forward_kernel,
        in_specs=[pl.BlockSpec(memory_space=pltpu.SMEM), hbm] + [vmem] * 4,
        out_specs=[vmem, vmem],
        out_shape=[
            jax.ShapeDtypeStruct((tokens, cols), F32),
            jax.ShapeDtypeStruct((4, tokens, depth), BF16),
        ],
        scratch_shapes=[pltpu.VMEM((4, tokens, depth), BF16), pltpu.SemaphoreType.DMA((8,))],
        compiler_params=PARAMS,
        cost_estimate=pl.CostEstimate(flops=8 * tokens * depth * cols, bytes_accessed=0, transcendentals=0),
        name="own_forward",
    )(at, acts, *weights)


def middle_kernel(*refs):
    held, parts, cot_ref, weights = refs[:2], refs[2:4], refs[4], refs[5:13]
    back_ref, outs, acc = refs[13], refs[14:21], refs[21]
    tokens, depth = held[0].shape[1:]
    half = depth // 2
    for i in range(4):
        for t in range(2):
            for n in range(0, tokens, TILE):
                where, near = pl.ds(t * tokens + n, TILE), pl.ds(n, TILE)
                term = sum(
                    jnp.dot(
                        held[t][i, near, pl.ds(h * half, half)],
                        weights[2 * i + h][...],
                        preferred_element_type=F32,
                    )
                    for h in range(2)
                )
                if i == 0:
                    acc[where, :] = parts[t][near, :] + term
                else:
                    acc[where, :] += term
    for n in range(0, 2 * tokens, TILE):
        where = pl.ds(n, TILE)
        for h in range(0, acc.shape[1], HEAD_DIM):
            head = pl.ds(h, HEAD_DIM)
            back_ref[where, head] = backprop(acc[where, head], cot_ref[where, head])
    for i in range(4):
        for n in range(0, depth, TILE):
            term = rows_dot(held[0][i, :, pl.ds(n, TILE)], back_ref[:tokens, :])
            term += rows_dot(held[1][i, :, pl.ds(n, TILE)], back_ref[tokens:, :])
            if i == 3:
                outs[6][pl.ds(n, TILE), :] = term
            else:
                out_ref = outs[2 * i + n // half]
                out_ref[pl.ds(n % half, TILE), :] = term.astype(out_ref.dtype)


def middle_call(held, parts, cot, weights):
    tokens, depth = held[0].shape[1:]
    cols = weights[0].shape[1]
    halves = (BF16, BF16, F32, BF16, BF16, F32)
    vmem = pl.BlockSpec(memory_space=pltpu.VMEM)
    return pl.pallas_call(
        middle_kernel,
        in_specs=[vmem] * 13,
        out_specs=[vmem] * 8,
        out_shape=[jax.ShapeDtypeStruct((2 * tokens, cols), BF16)]
        + [jax.ShapeDtypeStruct((depth // 2, cols), t) for t in halves]
        + [jax.ShapeDtypeStruct((depth, cols), F32)],
        scratch_shapes=[pltpu.VMEM((2 * tokens, cols), F32)],
        compiler_params=PARAMS,
        cost_estimate=pl.CostEstimate(flops=32 * tokens * depth * cols, bytes_accessed=0, transcendentals=0),
        name="middle",
    )(*held, *parts, cot, *weights)


def gradient_kernel(at_ref, own_ref, sib_ref, back_ref, *refs):
    outs, (acts, sems) = refs[:4], refs[4:]
    tokens = own_ref.shape[0]
    depth = acts.shape[2]

    def copy(i, t):
        start = pl.multiple_of(at_ref[i] * depth, depth)
        kept = acts.at[i, pl.ds(t * tokens, tokens), :]
        return pltpu.make_async_copy((own_ref, sib_ref)[t].at[:, pl.ds(start, depth)], kept, sems.at[i, t])

    for i in range(4):
        for t in range(2):
            copy(i, t).start()
    for i in range(4):
        for t in range(2):
            copy(i, t).wait()
        for n in range(0, depth, TILE):
            where = pl.ds(n, TILE)
            outs[i][where, :] = rows_dot(acts[i, :, where], back_ref[...]).astype(outs[i].dtype)


def gradient_call(at, own, sib, back, depth):
    tokens = own.shape[0]
    cols = back.shape[1]
    vmem = pl.BlockSpec(memory_space=pltpu.VMEM)
    hbm = pl.BlockSpec(memory_space=pltpu.HBM)
    return pl.pallas_call(
        gradient_kernel,
        in_specs=[pl.BlockSpec(memory_space=pltpu.SMEM), hbm, hbm, vmem],
        out_specs=[vmem] * 4,
        out_shape=[jax.ShapeDtypeStruct((depth, cols), t) for t in (BF16, BF16, BF16, F32)],
        scratch_shapes=[pltpu.VMEM((4, 2 * tokens, depth), BF16), pltpu.SemaphoreType.DMA((4, 2))],
        compiler_params=PARAMS,
        cost_estimate=pl.CostEstimate(
            flops=16 * tokens * depth * cols, bytes_accessed=0, transcendentals=0
        ),
        name="gradient",
    )(at, own, sib, back)


def block(value, index, size):
    return lax.dynamic_slice_in_dim(value, index * size, size, 0)


def rep_halves(value, bit):
    n = value.shape[0] // 2
    return block(value, bit, n), block(value, 1 - bit, n).astype(BF16)


def rep_rows(delta):
    y = lax.axis_index("rep") // NZL
    for bit in (1, 2):
        kept, given = rep_halves(delta, (y // bit) % 2)
        delta = kept, lax.ppermute(given, "rep", flip_perm(bit))
        if bit == 1:
            delta = delta[0] + delta[1].astype(F32)
    return delta


def rep_parts(pieces):
    part = pieces[0] + pieces[1].astype(F32)
    z = lax.axis_index("rep") % NZL
    m = part.shape[0] // NZL
    return [block(part, z, m)] + [rep_send(block(part, (z + k) % NZL, m), dz=k) for k in (1, 2, 3)]


def rep_average(pieces):
    total = pieces[0] + pieces[1] + pieces[3] + pieces[2]
    average = (total / (NY * NZL)).astype(BF16)
    return [average] + [rep_send(average, dz=-k) for k in (1, 2, 3)]


def ordered(pieces, index, holders):
    ring = jnp.stack(pieces)
    n = len(pieces)
    return jnp.concatenate([lax.dynamic_index_in_dim(ring, (k - index) % n, 0, keepdims=False) for k in holders])


def rep_gather(pieces):
    part = ordered(pieces, lax.axis_index("rep") % NZL, range(NZL))
    return [part] + [rep_send(part, dy=-k) for k in (1, 2, 3)]


def per_device(hidden, key_cotangent, local_weight, outer_delta, global_params, momentum, outer_step):
    f = lax.axis_index("fsdp")
    x, zh, core = f // 4, (f // 2) % 2, f % 2
    weight = local_weight[0]
    rows, width = weight.shape
    half = width // 2
    chip_rows = 2 * rows
    chip_of = lambda dx, dz: ((x + dx) % NX) * 2 + (zh ^ dz)

    def mine(a):
        return lax.dynamic_slice_in_dim(a, core * half, half, 1)

    def theirs(a):
        return lax.dynamic_slice_in_dim(a, (1 - core) * half, half, 1)

    def in_order(own, other):
        return jnp.where(core == 0, jnp.concatenate([own, other]), jnp.concatenate([other, own]))

    from_sib = send(jnp.concatenate([theirs(weight), theirs(key_cotangent)]), dc=1)
    cots = jnp.concatenate([mine(key_cotangent), from_sib[rows:]])
    here = in_order(mine(weight), from_sib[:rows])

    def spread(piece):
        return {0: piece, 3: send(piece, dx=1), 1: send(piece, dx=-1), 2: send(piece, dx=2)}

    away = send(here, dz=1)
    gathered = spread(here)
    far, right, left, away, here, cots, hidden, *blocks = tie(
        gathered[2], gathered[1], gathered[3], away, here, cots, hidden, *rep_rows(outer_delta[0])
    )
    gathered = [far, right, left, here]
    top, bottom = away[:rows], away[rows:]
    from_left, from_right = send(top, dx=1), send(bottom, dx=-1)
    from_left, *blocks = tie(from_left, *blocks)
    far = [send(from_left, dx=1), send(from_right, dx=-1)]
    distant = [*far, send(top, dx=-1), from_right, from_left, send(bottom, dx=1), top, bottom]
    hidden_sib = send(hidden, dc=1)
    at = lambda dz: jnp.stack([chip_of(dx, dz) for dx in ORDER]).astype(jnp.int32)
    both = jnp.concatenate([at(0), at(1)])
    part_own, held_own = forward_call(both, hidden, gathered)
    part_own, hidden_sib = tie(part_own, hidden_sib)
    part_sib, held_sib = forward_call(both, hidden_sib, gathered)
    parts, held = [part_own, part_sib], [held_own, held_sib]
    rest = tie(*parts, *held, *distant, *rep_parts(blocks))
    parts, held, rest = rest[:2], rest[2:4], rest[4:]
    distant, blocks = rest[:8], rest[8:]
    back, *found = middle_call(held, parts, cots, distant)

    def gather(found):
        return [send(found[0], dx=2), send(found[1], dx=1), send(found[2], dx=-1), found[3]]

    def total(found):
        found = [v.astype(F32) for v in found]
        return found[3] + (found[1] + found[2]) + found[0]

    up, down = send(found[0], dx=1), send(found[1], dx=-1)
    bottom, top = send(found[3], dx=1), send(found[4], dx=-1)
    up = send((found[2] + up.astype(F32)).astype(BF16), dx=1)
    down = send((found[5] + down.astype(F32)).astype(BF16), dx=-1)
    first = (up, down, bottom, top, found[6])
    back, *blocks = tie(back, *blocks)
    local = gradient_call(at(0), hidden, hidden_sib, back, chip_rows)
    rest = tie(*first, *local, *rep_average(blocks))
    (up, down, bottom, top, mid), local, blocks = rest[:5], rest[5:9], rest[9:]
    added = jnp.concatenate([up.astype(F32) + top.astype(F32), bottom.astype(F32) + down.astype(F32)])
    away = send((mid + added).astype(BF16), dz=1)
    local = gather(local)
    summed = [total([block(v, index, rows) for v in local]) for index in (core, 1 - core)]
    here, there, away, *blocks = tie(*summed, away, *rep_gather(blocks))
    finish = [v + block(away, index, rows).astype(F32) for v, index in zip((here, there), (core, 1 - core))]
    own, other = finish[0], send(finish[1], dc=1)
    average = ordered(blocks, lax.axis_index("rep") // NZL, (0, 2, 1, 3)).astype(F32)
    fragment = outer_step[0] % FRAGS
    old_moment = lax.dynamic_index_in_dim(momentum, fragment, 0, keepdims=False)
    old_params = lax.dynamic_index_in_dim(global_params, fragment, 0, keepdims=False)
    new_momentum = 0.9 * old_moment + average
    new_global = old_params - 0.7 * (average + 0.9 * new_momentum)
    grad = jnp.where(core == 0, jnp.concatenate([own, other], 1), jnp.concatenate([other, own], 1))

    return (grad[None], new_global, new_momentum)


def solution(mesh):
    in_specs = (
        P(("rep", "fsdp"), None),
        P(("rep", "fsdp"), None),
        P("rep", "fsdp", None),
        P("rep", "fsdp", None),
        P(None, "fsdp", None),
        P(None, "fsdp", None),
        P(),
    )
    out_specs = (P("rep", "fsdp", None), P("fsdp", None), P("fsdp", None))
    return jax.shard_map(
        per_device, mesh=mesh, in_specs=in_specs, out_specs=out_specs, check_vma=False
    )
```

```python
import jax
import jax.numpy as jnp
from jax import lax
from jax.experimental import pallas as pl
from jax.experimental.pallas import tpu as pltpu
from jax.sharding import PartitionSpec as P

HEAD_DIM = 128
FRAGS = 2
NX = 4
NY = 4
NZL = 4
F32 = jnp.float32
BF16 = jnp.bfloat16


def fsdp_perm(dx=0, dz=0, dc=0):
    pairs = []
    for f in range(16):
        x, z, c = f // 4, (f // 2) % 2, f % 2
        pairs.append((f, (((x + dx) % NX) * 2 + (z ^ dz)) * 2 + (c ^ dc)))
    return pairs


def rep_perm(dy=0, dz=0):
    pairs = []
    for r in range(16):
        y, z = r // NZL, r % NZL
        pairs.append((r, ((y + dy) % NY) * NZL + (z + dz) % NZL))
    return pairs


def flip_perm(bit):
    return [(r, (r // NZL ^ bit) * NZL + r % NZL) for r in range(16)]


def send(value, **kw):
    return lax.ppermute(value, "fsdp", fsdp_perm(**kw))


def rep_send(value, **kw):
    return lax.ppermute(value, "rep", rep_perm(**kw))


def tie(*values):
    return lax.optimization_barrier(values)


ORDER = (2, 1, 3, 0)
TILE = 256
PARAMS = pltpu.CompilerParams(vmem_limit_bytes=22 * 1024 * 1024)


def rows_dot(a, b):
    return lax.dot_general(a, b, (((0,), (0,)), ((), ())), preferred_element_type=F32)


def backprop(projected, incoming):
    inverse_rms = lax.rsqrt(jnp.mean(projected * projected, axis=-1, keepdims=True) + 1e-06)
    normed = projected * inverse_rms
    incoming = incoming.astype(F32)
    along = jnp.mean(incoming * normed, axis=-1, keepdims=True)
    return (inverse_rms * (incoming - normed * along)).astype(BF16)


def forward_kernel(at_ref, acts_ref, *refs):
    weights, (out_ref, held, acts, sems) = refs[:4], refs[4:]
    depth = held.shape[2]

    def copy(i):
        start = pl.multiple_of(at_ref[i] * depth, depth)
        kept = (acts if i < 4 else held).at[i % 4]
        return pltpu.make_async_copy(acts_ref.at[:, pl.ds(start, depth)], kept, sems.at[i])

    for i in range(8):
        copy(i).start()
    for i in range(4):
        copy(i).wait()
        for n in range(0, out_ref.shape[0], TILE):
            where = pl.ds(n, TILE)
            term = jnp.dot(acts[i, where, :], weights[i][...], preferred_element_type=F32)
            if i == 0:
                out_ref[where, :] = term
            else:
                out_ref[where, :] += term
    for i in range(4, 8):
        copy(i).wait()


def forward_call(at, acts, weights):
    tokens = acts.shape[0]
    depth, cols = weights[0].shape
    vmem = pl.BlockSpec(memory_space=pltpu.VMEM)
    hbm = pl.BlockSpec(memory_space=pltpu.HBM)
    return pl.pallas_call(
        forward_kernel,
        in_specs=[pl.BlockSpec(memory_space=pltpu.SMEM), hbm] + [vmem] * 4,
        out_specs=[vmem, vmem],
        out_shape=[
            jax.ShapeDtypeStruct((tokens, cols), F32),
            jax.ShapeDtypeStruct((4, tokens, depth), BF16),
        ],
        scratch_shapes=[pltpu.VMEM((4, tokens, depth), BF16), pltpu.SemaphoreType.DMA((8,))],
        compiler_params=PARAMS,
        cost_estimate=pl.CostEstimate(flops=8 * tokens * depth * cols, bytes_accessed=0, transcendentals=0),
        name="own_forward",
    )(at, acts, *weights)


def middle_kernel(*refs):
    held, parts, cot_ref, weights = refs[:2], refs[2:4], refs[4], refs[5:13]
    back_ref, outs, acc = refs[13], refs[14:21], refs[21]
    tokens, depth = held[0].shape[1:]
    half = depth // 2
    for i in range(4):
        for t in range(2):
            for n in range(0, tokens, TILE):
                where, near = pl.ds(t * tokens + n, TILE), pl.ds(n, TILE)
                term = sum(
                    jnp.dot(
                        held[t][i, near, pl.ds(h * half, half)],
                        weights[2 * i + h][...],
                        preferred_element_type=F32,
                    )
                    for h in range(2)
                )
                if i == 0:
                    acc[where, :] = parts[t][near, :] + term
                else:
                    acc[where, :] += term
    for n in range(0, 2 * tokens, TILE):
        where = pl.ds(n, TILE)
        for h in range(0, acc.shape[1], HEAD_DIM):
            head = pl.ds(h, HEAD_DIM)
            back_ref[where, head] = backprop(acc[where, head], cot_ref[where, head])
    for i in range(4):
        for n in range(0, depth, TILE):
            term = rows_dot(held[0][i, :, pl.ds(n, TILE)], back_ref[:tokens, :])
            term += rows_dot(held[1][i, :, pl.ds(n, TILE)], back_ref[tokens:, :])
            if i == 3:
                outs[6][pl.ds(n, TILE), :] = term
            else:
                out_ref = outs[2 * i + n // half]
                out_ref[pl.ds(n % half, TILE), :] = term.astype(out_ref.dtype)


def middle_call(held, parts, cot, weights):
    tokens, depth = held[0].shape[1:]
    cols = weights[0].shape[1]
    halves = (BF16, BF16, F32, BF16, BF16, F32)
    vmem = pl.BlockSpec(memory_space=pltpu.VMEM)
    return pl.pallas_call(
        middle_kernel,
        in_specs=[vmem] * 13,
        out_specs=[vmem] * 8,
        out_shape=[jax.ShapeDtypeStruct((2 * tokens, cols), BF16)]
        + [jax.ShapeDtypeStruct((depth // 2, cols), t) for t in halves]
        + [jax.ShapeDtypeStruct((depth, cols), F32)],
        scratch_shapes=[pltpu.VMEM((2 * tokens, cols), F32)],
        compiler_params=PARAMS,
        cost_estimate=pl.CostEstimate(flops=32 * tokens * depth * cols, bytes_accessed=0, transcendentals=0),
        name="middle",
    )(*held, *parts, cot, *weights)


def gradient_kernel(at_ref, own_ref, sib_ref, back_ref, *refs):
    outs, (acts, sems) = refs[:4], refs[4:]
    tokens = own_ref.shape[0]
    depth = acts.shape[2]

    def copy(i, t):
        start = pl.multiple_of(at_ref[i] * depth, depth)
        kept = acts.at[i, pl.ds(t * tokens, tokens), :]
        return pltpu.make_async_copy((own_ref, sib_ref)[t].at[:, pl.ds(start, depth)], kept, sems.at[i, t])

    for i in range(4):
        for t in range(2):
            copy(i, t).start()
    for i in range(4):
        for t in range(2):
            copy(i, t).wait()
        for n in range(0, depth, TILE):
            where = pl.ds(n, TILE)
            outs[i][where, :] = rows_dot(acts[i, :, where], back_ref[...]).astype(outs[i].dtype)


def gradient_call(at, own, sib, back, depth):
    tokens = own.shape[0]
    cols = back.shape[1]
    vmem = pl.BlockSpec(memory_space=pltpu.VMEM)
    hbm = pl.BlockSpec(memory_space=pltpu.HBM)
    return pl.pallas_call(
        gradient_kernel,
        in_specs=[pl.BlockSpec(memory_space=pltpu.SMEM), hbm, hbm, vmem],
        out_specs=[vmem] * 4,
        out_shape=[jax.ShapeDtypeStruct((depth, cols), t) for t in (BF16, BF16, BF16, F32)],
        scratch_shapes=[pltpu.VMEM((4, 2 * tokens, depth), BF16), pltpu.SemaphoreType.DMA((4, 2))],
        compiler_params=PARAMS,
        cost_estimate=pl.CostEstimate(
            flops=16 * tokens * depth * cols, bytes_accessed=0, transcendentals=0
        ),
        name="gradient",
    )(at, own, sib, back)


def block(value, index, size):
    return lax.dynamic_slice_in_dim(value, index * size, size, 0)


def rep_halves(value, bit):
    n = value.shape[0] // 2
    return block(value, bit, n), block(value, 1 - bit, n).astype(BF16)


def rep_rows(delta):
    y = lax.axis_index("rep") // NZL
    for bit in (1, 2):
        kept, given = rep_halves(delta, (y // bit) % 2)
        delta = kept, lax.ppermute(given, "rep", flip_perm(bit))
        if bit == 1:
            delta = delta[0] + delta[1].astype(F32)
    return delta


def rep_parts(pieces):
    part = pieces[0] + pieces[1].astype(F32)
    z = lax.axis_index("rep") % NZL
    m = part.shape[0] // NZL
    return [block(part, z, m)] + [rep_send(block(part, (z + k) % NZL, m), dz=k) for k in (1, 2, 3)]


def rep_average(pieces):
    total = pieces[0] + pieces[1] + pieces[3] + pieces[2]
    average = (total / (NY * NZL)).astype(BF16)
    return [average] + [rep_send(average, dz=-k) for k in (1, 2, 3)]


def ordered(pieces, index, holders):
    ring = jnp.stack(pieces)
    n = len(pieces)
    return jnp.concatenate([lax.dynamic_index_in_dim(ring, (k - index) % n, 0, keepdims=False) for k in holders])


def rep_gather(pieces):
    part = ordered(pieces, lax.axis_index("rep") % NZL, range(NZL))
    return [part] + [rep_send(part, dy=-k) for k in (1, 2, 3)]


def per_device(hidden, key_cotangent, local_weight, outer_delta, global_params, momentum, outer_step):
    f = lax.axis_index("fsdp")
    x, zh, core = f // 4, (f // 2) % 2, f % 2
    weight = local_weight[0]
    rows, width = weight.shape
    half = width // 2
    chip_rows = 2 * rows
    chip_of = lambda dx, dz: ((x + dx) % NX) * 2 + (zh ^ dz)

    def mine(a):
        return lax.dynamic_slice_in_dim(a, core * half, half, 1)

    def theirs(a):
        return lax.dynamic_slice_in_dim(a, (1 - core) * half, half, 1)

    def in_order(own, other):
        return jnp.where(core == 0, jnp.concatenate([own, other]), jnp.concatenate([other, own]))

    here = in_order(mine(weight), send(theirs(weight), dc=1))
    here, given = tie(here, theirs(key_cotangent))
    cots = jnp.concatenate([mine(key_cotangent), send(given, dc=1)])

    def spread(piece):
        return {0: piece, 3: send(piece, dx=1), 1: send(piece, dx=-1), 2: send(piece, dx=2)}

    away = send(here, dz=1)
    gathered = spread(here)
    far, right, left, away, here, cots, hidden, *blocks = tie(
        gathered[2], gathered[1], gathered[3], away, here, cots, hidden, *rep_rows(outer_delta[0])
    )
    gathered = [far, right, left, here]
    top, bottom = away[:rows], away[rows:]
    from_left, from_right = send(top, dx=1), send(bottom, dx=-1)
    from_left, *blocks = tie(from_left, *blocks)
    far = [send(from_left, dx=1), send(from_right, dx=-1)]
    distant = [*far, send(top, dx=-1), from_right, from_left, send(bottom, dx=1), top, bottom]
    hidden_sib = send(hidden, dc=1)
    at = lambda dz: jnp.stack([chip_of(dx, dz) for dx in ORDER]).astype(jnp.int32)
    both = jnp.concatenate([at(0), at(1)])
    part_own, held_own = forward_call(both, hidden, gathered)
    part_own, hidden_sib = tie(part_own, hidden_sib)
    part_sib, held_sib = forward_call(both, hidden_sib, gathered)
    parts, held = [part_own, part_sib], [held_own, held_sib]
    rest = tie(*parts, *held, *distant, *rep_parts(blocks))
    parts, held, rest = rest[:2], rest[2:4], rest[4:]
    distant, blocks = rest[:8], rest[8:]
    back, *found = middle_call(held, parts, cots, distant)

    def gather(found):
        return [send(found[0], dx=2), send(found[1], dx=1), send(found[2], dx=-1), found[3]]

    def total(found):
        found = [v.astype(F32) for v in found]
        return found[3] + (found[1] + found[2]) + found[0]

    up, down = send(found[0], dx=1), send(found[1], dx=-1)
    bottom, top = send(found[3], dx=1), send(found[4], dx=-1)
    up = send((found[2] + up.astype(F32)).astype(BF16), dx=1)
    down = send((found[5] + down.astype(F32)).astype(BF16), dx=-1)
    first = (up, down, bottom, top, found[6])
    back, *blocks = tie(back, *blocks)
    local = gradient_call(at(0), hidden, hidden_sib, back, chip_rows)
    rest = tie(*first, *local, *rep_average(blocks))
    (up, down, bottom, top, mid), local, blocks = rest[:5], rest[5:9], rest[9:]
    added = jnp.concatenate([up.astype(F32) + top.astype(F32), bottom.astype(F32) + down.astype(F32)])
    away = send((mid + added).astype(BF16), dz=1)
    local = gather(local)
    summed = [total([block(v, index, rows) for v in local]) for index in (core, 1 - core)]
    here, there, away, *blocks = tie(*summed, away, *rep_gather(blocks))
    finish = [v + block(away, index, rows).astype(F32) for v, index in zip((here, there), (core, 1 - core))]
    own, other = finish[0], send(finish[1], dc=1)
    average = ordered(blocks, lax.axis_index("rep") // NZL, (0, 2, 1, 3)).astype(F32)
    fragment = outer_step[0] % FRAGS
    old_moment = lax.dynamic_index_in_dim(momentum, fragment, 0, keepdims=False)
    old_params = lax.dynamic_index_in_dim(global_params, fragment, 0, keepdims=False)
    new_momentum = 0.9 * old_moment + average
    new_global = old_params - 0.7 * (average + 0.9 * new_momentum)
    grad = jnp.where(core == 0, jnp.concatenate([own, other], 1), jnp.concatenate([other, own], 1))

    return (grad[None], new_global, new_momentum)


def solution(mesh):
    in_specs = (
        P(("rep", "fsdp"), None),
        P(("rep", "fsdp"), None),
        P("rep", "fsdp", None),
        P("rep", "fsdp", None),
        P(None, "fsdp", None),
        P(None, "fsdp", None),
        P(),
    )
    out_specs = (P("rep", "fsdp", None), P("fsdp", None), P("fsdp", None))
    return jax.shard_map(
        per_device, mesh=mesh, in_specs=in_specs, out_specs=out_specs, check_vma=False
    )
```
